32 devices in a mesh: tm: 4 (over y, core), fiber: 8 (over z, x).
Axes of the slice: x: 2, y: 2, z: 4, core: 2. Of those that a mesh axis runs over, the one named last changes fastest.
Arguments:
- waveform: bfloat16 [4096, 8192], P('fiber', 'tm'), may hold values from -6 to 6
- filters: bfloat16 [512, 256], replicated, may hold values from -0.25 to 0.25
- channel_section: int32 [4096], replicated, may hold values from 0 to 127, never falling along the last dimension, each value on 1 to 64 neighbouring positions
- section_bank: int32 [128, 8], replicated, may hold values from 0 to 1
- conv_bank: bfloat16 [2, 8, 3, 3, 32, 32], P(None, 'fiber'), may hold values from -0.375 to 0.375
Outputs:
- events: bfloat16 [4096, 256, 64], P('tm', 'fiber')
The draws below stay inside these ranges and needn't reach their ends.
Inputs may be any that keep to these rules, and one draw needn't show every extreme that they name: `channel_section`: never falls along the channels; every section has 1 to 64 channels.
All inputs are finite; a program needn't handle non-finite values.
Results may differ from the reference program's by a relative error of at most 0.005.
Values may be sent and summed in bfloat16 or wider, within the bound.
A program may use at most 128 MiB of HBM per device.

```python
import math
import jax
import jax.numpy as jnp
import numpy as np
from jax import lax

TAPS = 512
HOP = 128
FILTERS = 256
GW = 32
BANKS = 2
SEC_MOST = 64
CHANNELS = 4096
SAMPLES = 8192
FRAMES = 64
GROUPS = 8
SECTIONS = 128


def plant(values, own_key, low, high):
    longest = values.shape.index(max(values.shape))
    spots = []
    for shift in (0, 1):
        where = [jax.random.randint(jax.random.fold_in(own_key, axis), (), 0, length) for axis, length in enumerate(values.shape)]
        where[longest] = (where[longest] + shift) % values.shape[longest]
        spots.append(tuple(where))
    return values.at[spots[0]].set(low).at[spots[1]].set(high)


def block_scale(rng, shape, cuts, least, high):
    def one(position, parts):
        steps = jax.random.uniform(jax.random.fold_in(jax.random.fold_in(rng, 6), position), (parts,), jnp.float32, least / len(cuts), high / len(cuts))
        return jnp.repeat(jnp.exp(steps), shape[position] // parts).reshape((-1,) + (1,) * (len(shape) - position - 1))

    factor_of = one(*cuts[0])
    for cut in cuts[1:]:
        factor_of = factor_of * one(*cut)
    return factor_of


def profile(number_of, total, bound, skew):
    portions = [(1 << 20) // math.isqrt(grade ** skew) + 1 for grade in range(2, number_of + 1)]
    rest, counts = total - bound - (number_of - 1), [1] * (number_of - 1)
    while rest > 0:
        free = [i for i in range(number_of - 1) if counts[i] < bound]
        pool, budget = sum([portions[i] for i in free]), rest
        for i in free:
            extra = min(bound - counts[i], max(1, budget * portions[i] // pool), rest)
            counts[i] = counts[i] + extra
            rest = rest - extra
    return np.array([bound] + counts)


def uneven(rng, amount, total, reach, skew):
    if amount == 2:
        one = jax.random.randint(rng, (), max(1, total - reach), min(reach, total - 1) + 1)
        return jnp.stack([one, total - one])
    lengths = jnp.asarray(profile(amount, total, reach, skew), jnp.int32)
    pairs = (amount - 1) // 2
    giver, taker = lengths[1:1 + 2 * pairs:2], lengths[2:2 + 2 * pairs:2]
    margin = jnp.minimum(giver - 1, reach - taker)
    passed = jax.random.randint(jax.random.fold_in(rng, 1), (pairs,), 0, 1 << 20) % (margin + 1)
    lengths = lengths.at[1:1 + 2 * pairs:2].set(giver - passed).at[2:2 + 2 * pairs:2].set(taker + passed)
    return lengths[jax.random.permutation(jax.random.fold_in(rng, 2), amount)]


def centred(own_key, extent, spread, limit, split=(), kind=jnp.bfloat16):
    values = jax.random.normal(own_key, extent, jnp.float32) * spread
    if len(split) > 0:
        values = block_scale(own_key, extent, split, -0.22, 0.18) * values
    return jnp.clip(values, min=-limit, max=limit).astype(kind)


def setup_inputs(seed: int = 0) -> dict:
    arg_keys = jax.random.split(jax.random.key(seed), 6)
    waveform = centred(arg_keys[0], (CHANNELS, SAMPLES), 1.0, 6.0, ((0, 8), (1, 4)))
    filters = centred(arg_keys[1], (TAPS, FILTERS), TAPS ** -0.5, 0.25)
    channel_section = jnp.searchsorted(jnp.cumsum(uneven(arg_keys[2], SECTIONS, CHANNELS, SEC_MOST, 1)), jnp.arange(CHANNELS), side="right").astype(jnp.int32)
    section_bank = plant(jax.random.randint(arg_keys[3], (SECTIONS, GROUPS), 0, BANKS), jax.random.fold_in(arg_keys[3], 1), 0, BANKS - 1).astype(jnp.int32)
    conv_bank = centred(arg_keys[4], (BANKS, GROUPS, 3, 3, GW, GW), (9 * GW) ** -0.5, 0.375, ((1, 8),))
    return dict(waveform=waveform, filters=filters, channel_section=channel_section, section_bank=section_bank, conv_bank=conv_bank)


def filter_rows(wave_rows, filt):
    count = wave_rows.shape[0]
    blocks = wave_rows.astype(jnp.float32).reshape(count, FRAMES + TAPS // HOP - 1, HOP)
    total = jnp.zeros((count, FRAMES, FILTERS), jnp.float32)
    for k in range(TAPS // HOP):
        total = total + jnp.einsum('cfh,hj->cfj', blocks[:, k:k + FRAMES], filt[k * HOP:(k + 1) * HOP], precision=lax.Precision.HIGHEST)
    return total.astype(jnp.bfloat16)


def reference(waveform, filters, channel_section, section_bank, conv_bank):
    wave = jnp.pad(waveform, ((0, 0), (0, TAPS - HOP)))
    filt = filters.astype(jnp.float32)
    rows = math.gcd(CHANNELS, 64)
    nblock = CHANNELS // rows
    feats = lax.map(lambda i: filter_rows(lax.dynamic_slice_in_dim(wave, i * rows, rows, 0), filt), jnp.arange(nblock, dtype=jnp.int32))
    feats = feats.reshape(CHANNELS, FRAMES, GROUPS, GW).transpose(0, 2, 3, 1)
    padded = jnp.pad(feats, ((1, 1), (0, 0), (0, 0), (1, 1)))
    edge = jnp.array([-1], jnp.int32)
    sec = jnp.concatenate([edge, channel_section.astype(jnp.int32), edge])
    same_lo = (sec[:-2] == sec[1:-1]).astype(jnp.float32)
    same_hi = (sec[2:] == sec[1:-1]).astype(jnp.float32)
    choose = section_bank[channel_section]
    pick_all = (choose[:, :, None] == jnp.arange(BANKS, dtype=jnp.int32)[None, None, :]).astype(jnp.float32)
    weights = conv_bank.astype(jnp.float32)

    def conv_block(i):
        start = (i * rows).astype(jnp.int32)
        xs = lax.dynamic_slice_in_dim(padded, start, rows + 2, 0).astype(jnp.float32)
        low = lax.dynamic_slice_in_dim(same_lo, start, rows, 0)
        high = lax.dynamic_slice_in_dim(same_hi, start, rows, 0)
        pick = lax.dynamic_slice_in_dim(pick_all, start, rows, 0)
        acc = jnp.zeros((rows, GROUPS, BANKS, GW, FRAMES), jnp.float32)
        for d in range(3):
            part = xs[d:d + rows]
            if d == 0:
                part = part * low[:, None, None, None]
            if d == 2:
                part = part * high[:, None, None, None]
            for e in range(3):
                acc = acc + jnp.einsum('bgoi,cgit->cgbot', weights[:, :, d, e], part[..., e:e + FRAMES], precision=lax.Precision.HIGHEST)
        out = jnp.sum(acc * pick[:, :, :, None, None], axis=2)
        return out.astype(jnp.bfloat16).reshape(rows, FILTERS, FRAMES)

    events = lax.map(conv_block, jnp.arange(nblock, dtype=jnp.int32))
    return events.reshape(CHANNELS, FILTERS, FRAMES)
```

```python
import functools

import jax
import jax.numpy as jnp
from jax import lax
from jax.experimental import pallas as pl
from jax.experimental.pallas import tpu as pltpu
from jax.sharding import PartitionSpec as P

HOP = 128
GW = 32
LANES = 128
MESH = pl.DeviceIdType.MESH
NT_DIMS = (((1,), (1,)), ((), ()))


def kernel(nt, nf, wave, filt_t, bands, section, table, out, w, ft, s, r1, x, marks,
           load_sem, rim_sem, s1_send, s1_recv, s2_send, x_recv, h_send, h_recv):
    t = lax.axis_index("tm")
    f = lax.axis_index("fiber")
    ch_dev, samp = wave.shape
    rim = w.shape[1] - samp
    span = ft.shape[1]
    hops = (span - rim) // HOP
    blk = hops * GW
    nb = samp // (HOP * hops)
    rows = out.shape[2]
    q = min(rows, ch_dev)
    ndc, nsub = rows // q, ch_dev // q
    part = nb * blk
    half = nf // 2

    load = pltpu.make_async_copy(wave, w.at[:, pl.ds(0, samp)], load_sem)
    load.start()

    barrier = pltpu.get_barrier_semaphore()
    for k in range(1, nf):
        pl.semaphore_signal(barrier, inc=1, device_id=(t, f ^ k), device_id_type=MESH)
    for j in range(1, nt):
        pl.semaphore_signal(barrier, inc=1, device_id=(lax.rem(t + j, nt), f), device_id_type=MESH)
    pl.semaphore_wait(barrier, nf - 1 + nt - 1)

    def rim_copy(to):
        return pltpu.make_async_remote_copy(
            src_ref=wave.at[:, pl.ds(0, rim)], dst_ref=w.at[:, pl.ds(samp, rim)],
            send_sem=rim_sem.at[0], recv_sem=rim_sem.at[1],
            device_id=(to, f), device_id_type=MESH)

    @pl.when(t > 0)
    def _():
        rim_copy(t - 1).start()

    @pl.when(t == nt - 1)
    def _():
        w[:, samp:] = jnp.zeros((ch_dev, rim), w.dtype)

    taps = filt_t.shape[1]
    ft[...] = jnp.zeros(ft.shape, ft.dtype)
    for g in range(nf):
        for h in range(hops):
            ft[g * blk + h * GW:g * blk + (h + 1) * GW, h * HOP:h * HOP + taps] = (
                filt_t[g * GW:(g + 1) * GW, :])
    load.wait()

    def rowsof(g, b):
        return s.at[g, pl.ds(b * blk, blk), :]

    def first(k, b):
        g = f ^ k
        return pltpu.make_async_remote_copy(
            src_ref=rowsof(g, b), dst_ref=r1.at[f, pl.ds(b * blk, blk), :],
            send_sem=s1_send.at[k, b], recv_sem=s1_recv.at[k, b],
            device_id=(t, g), device_id_type=MESH)

    def features(b, side):
        lo = pl.multiple_of(side * (half * blk), half * blk)
        res = lax.dot_general(
            ft[pl.ds(lo, half * blk), :], w[:, b * hops * HOP:b * hops * HOP + span], NT_DIMS,
            preferred_element_type=jnp.float32).astype(s.dtype)
        for g in range(half):
            s[side * half + g, b * blk:(b + 1) * blk, :] = res[g * blk:(g + 1) * blk]

    mine = f // half
    for b in range(nb):
        if b == nb - 1:
            @pl.when(t < nt - 1)
            def _():
                rim_copy(t).wait_recv()
        features(b, 1 - mine)
        for k in range(nf - 1, half - 1, -1):
            first(k, b).start()
    for b in range(nb):
        features(b, mine)
        for k in range(half - 1, 0, -1):
            first(k, b).start()

    chans = section.shape[1]
    sec = section[...]
    lane = lax.broadcasted_iota(jnp.int32, (1, chans), 1)
    low = jnp.logical_and(pltpu.roll(sec, 1, 1) == sec, lane > 0)
    high = jnp.logical_and(pltpu.roll(sec, chans - 1, 1) == sec, lane < chans - 1)
    marks[0:1, :] = low.astype(jnp.float32)
    marks[1:2, :] = high.astype(jnp.float32)
    tab = table[...]
    here = lax.broadcasted_iota(jnp.int32, tab.shape, 0) == f
    column = jnp.sum(jnp.where(here, tab, 0).astype(jnp.float32), axis=0, keepdims=True)
    wide = min(chans, 512)
    for c in range(0, chans, wide):
        hot = lax.broadcasted_iota(jnp.int32, (tab.shape[1], wide), 0) == sec[:, c:c + wide]
        marks[2:3, c:c + wide] = jnp.dot(
            column, hot.astype(jnp.float32), preferred_element_type=jnp.float32)
    total = x.shape[0]
    x[0:GW, :] = jnp.zeros((GW, x.shape[1]), x.dtype)
    x[total - GW:total, :] = jnp.zeros((GW, x.shape[1]), x.dtype)

    @pl.when(t == 0)
    def _():
        x[GW:total - GW, 0:LANES] = jnp.zeros((total - 2 * GW, LANES), x.dtype)

    @pl.when(t == nt - 1)
    def _():
        x[GW:total - GW, LANES + rows:] = jnp.zeros((total - 2 * GW, LANES), x.dtype)

    def place(source_t, slot, b):
        return x.at[pl.ds(GW + source_t * part + b * blk, blk), pl.ds(LANES + slot * q, q)]

    def second(k, b, i):
        fb = f ^ k
        gc = fb * nsub + i
        to = gc // ndc
        slot = gc % ndc
        src = (s if k == 0 else r1).at[fb, pl.ds(b * blk, blk), pl.ds(i * q, q)]
        dst = place(t, slot, b)
        sem = x_recv.at[t, slot, b]
        return to, pltpu.make_async_copy(src, dst, sem), pltpu.make_async_remote_copy(
            src_ref=src, dst_ref=dst, send_sem=s2_send.at[k, b, i], recv_sem=sem,
            device_id=(to, f), device_id_type=MESH)

    def halo(k, i, upper):
        fb = f ^ k
        gc = fb * nsub + i
        owner = gc // ndc
        to = owner + 1 if upper else owner - 1
        edge = lax.rem(gc, ndc) == (ndc - 1 if upper else 0)
        there = jnp.logical_and(edge, jnp.logical_and(to >= 0, to < nt))
        column = (i + 1) * q - LANES if upper else i * q
        src = (s if k == 0 else r1).at[fb, :, pl.ds(column, LANES)]
        dst = x.at[pl.ds(GW + t * part, part), pl.ds(0 if upper else LANES + rows, LANES)]
        sem = h_recv.at[t, 0 if upper else 1]
        return there, to, pltpu.make_async_copy(src, dst, sem), pltpu.make_async_remote_copy(
            src_ref=src, dst_ref=dst, send_sem=h_send.at[k, i, 0 if upper else 1], recv_sem=sem,
            device_id=(to, f), device_id_type=MESH)

    order = list(range(nf - 1, half - 1, -1)), list(range(half - 1, -1, -1))
    for ks in order:
        for b in range(nb):
            for k in ks:
                if k > 0:
                    first(k, b).wait_recv()
                for i in range(nsub):
                    to, local, remote = second(k, b, i)

                    @pl.when(to == t)
                    def _():
                        local.start()

                    @pl.when(to != t)
                    def _():
                        remote.start()

                    if b == nb - 1:
                        for upper in (True, False):
                            there, to, local, remote = halo(k, i, upper)

                            @pl.when(jnp.logical_and(there, to == t))
                            def _():
                                local.start()

                            @pl.when(jnp.logical_and(there, to != t))
                            def _():
                                remote.start()

    for source in range(nt):
        for slot in range(ndc):
            for b in range(nb):
                ref = place(source, slot, b)
                pltpu.make_async_copy(ref, ref, x_recv.at[source, slot, b]).wait()
        for side, there in ((0, t > 0), (1, t < nt - 1)):
            ref = x.at[pl.ds(GW + source * part, part), pl.ds(side * (LANES + rows), LANES)]

            @pl.when(there)
            def _():
                pltpu.make_async_copy(ref, ref, h_recv.at[source, side]).wait()

    run = 8
    deep = (run + 2) * GW
    lb = min(256, rows)
    ow = out.shape[0]
    pack = 2 * run
    start = t * rows

    def conv(step, carry):
        tt = step // (rows // lb)
        l0 = pl.multiple_of((step % (rows // lb)) * lb, lb)
        here = pl.ds(pl.multiple_of(start + l0, lb), lb)
        low, high, pick = marks[0:1, here], marks[1:2, here], marks[2:3, here]
        both = []
        for h in range(2):
            top = pl.multiple_of(tt * (pack * GW) + h * (run * GW), run * GW)
            block = x[pl.ds(top, deep), pl.ds(l0, lb + 2 * LANES)]
            wide = block.astype(jnp.float32)
            before = pltpu.roll(wide, 1, 1)[:, LANES:LANES + lb] * low
            after = pltpu.roll(wide, lb + 2 * LANES - 1, 1)[:, LANES:LANES + lb] * high
            depth = jnp.concatenate(
                [before.astype(x.dtype), block[:, LANES:LANES + lb], after.astype(x.dtype)], axis=0)
            acc = jnp.dot(bands[...], depth, preferred_element_type=jnp.float32)
            n = acc.shape[0] // 2
            res = acc[:n]
            res = jnp.where(pick == 1.0, acc[n:], res)
            both.append(res.reshape(ow, run, lb))
        out[:, pl.ds(pl.multiple_of(tt * pack, pack), pack), pl.ds(l0, lb)] = (
            jnp.concatenate(both, axis=1).astype(out.dtype))
        return carry

    lax.fori_loop(0, (out.shape[1] // pack) * (rows // lb), conv, 0)

    @pl.when(t > 0)
    def _():
        rim_copy(t - 1).wait_send()

    for k in range(nf):
        for b in range(nb):
            if k > 0:
                first(k, b).wait_send()
            for i in range(nsub):
                to, _, remote = second(k, b, i)

                @pl.when(to != t)
                def _():
                    remote.wait_send()
        for i in range(nsub):
            for upper in (True, False):
                there, to, _, remote = halo(k, i, upper)

                @pl.when(jnp.logical_and(there, to != t))
                def _():
                    remote.wait_send()


def shards(nt, nf, waveform, filters, channel_section, section_bank, conv_bank):
    ch_dev, samp = waveform.shape
    taps, nfilt = filters.shape
    rim = taps - HOP
    hops = LANES // GW
    span = rim + hops * HOP
    nb = samp // (HOP * hops)
    blk = hops * GW
    rows = ch_dev * nf // nt
    frames = samp // HOP * nt
    q = min(rows, ch_dev)
    ndc, nsub = rows // q, ch_dev // q
    banks = conv_bank.shape[0]
    run = 8
    base = conv_bank[:, 0].transpose(0, 3, 1, 2, 4).reshape(banks * GW, 3, 3 * GW)
    bands = jnp.stack(
        [jnp.pad(base, ((0, 0), (0, 0), (r * GW, (run - 1 - r) * GW))) for r in range(run)], axis=1
    ).reshape(banks * GW * run, 3 * (run + 2) * GW)
    dt = waveform.dtype
    vmem = pl.BlockSpec(memory_space=pltpu.VMEM)
    dma = pltpu.SemaphoreType.DMA
    events = pl.pallas_call(
        functools.partial(kernel, nt, nf),
        out_shape=jax.ShapeDtypeStruct((GW, frames, rows), dt),
        in_specs=[pl.BlockSpec(memory_space=pl.ANY)] + [vmem] * 4,
        out_specs=vmem,
        scratch_shapes=[
            pltpu.VMEM((ch_dev, samp + rim), dt),
            pltpu.VMEM((nf * blk, span), dt),
            pltpu.VMEM((nf, nb * blk, ch_dev), dt),
            pltpu.VMEM((nf, nb * blk, ch_dev), dt),
            pltpu.VMEM((frames * GW + 2 * GW, rows + 2 * LANES), dt),
            pltpu.VMEM((8, channel_section.shape[0]), jnp.float32),
            dma, dma((2,)), dma((nf, nb)), dma((nf, nb)), dma((nf, nb, nsub)),
            dma((nt, ndc, nb)), dma((nf, nsub, 2)), dma((nt, 2)),
        ],
        compiler_params=pltpu.CompilerParams(
            collective_id=0, has_side_effects=True, vmem_limit_bytes=56 * 1024 * 1024),
    )(waveform, filters.T, bands, channel_section[None, :], section_bank.T)
    return events.transpose(2, 0, 1)


def solution(mesh):
    placed = (P("fiber", "tm"), P(), P(), P(), P(None, "fiber", None, None, None, None))
    return jax.shard_map(
        functools.partial(shards, mesh.shape["tm"], mesh.shape["fiber"]), mesh=mesh,
        in_specs=placed, out_specs=P("tm", "fiber", None), check_vma=False
    )
```

```python
import functools

import jax
import jax.numpy as jnp
from jax import lax
from jax.experimental import pallas as pl
from jax.experimental.pallas import tpu as pltpu
from jax.sharding import PartitionSpec as P

HOP = 128
GW = 32
LANES = 128
MESH = pl.DeviceIdType.MESH
NT_DIMS = (((1,), (1,)), ((), ()))


def kernel(nt, nf, wave, filt_t, bands, section, table, out, w, ft, s, r1, x, marks,
           load_sem, rim_sem, s1_send, s1_recv, s2_send, x_recv, h_send, h_recv):
    t = lax.axis_index("tm")
    f = lax.axis_index("fiber")
    ch_dev, samp = wave.shape
    rim = w.shape[1] - samp
    span = ft.shape[1]
    hops = (span - rim) // HOP
    blk = hops * GW
    nb = samp // (HOP * hops)
    rows = out.shape[2]
    q = min(rows, ch_dev)
    ndc, nsub = rows // q, ch_dev // q
    part = nb * blk
    half = nf // 2

    load = pltpu.make_async_copy(wave, w.at[:, pl.ds(0, samp)], load_sem)
    load.start()

    barrier = pltpu.get_barrier_semaphore()
    for k in range(1, nf):
        pl.semaphore_signal(barrier, inc=1, device_id=(t, f ^ k), device_id_type=MESH)
    for j in range(1, nt):
        pl.semaphore_signal(barrier, inc=1, device_id=(lax.rem(t + j, nt), f), device_id_type=MESH)
    pl.semaphore_wait(barrier, nf - 1 + nt - 1)

    def rim_copy(to):
        return pltpu.make_async_remote_copy(
            src_ref=wave.at[:, pl.ds(0, rim)], dst_ref=w.at[:, pl.ds(samp, rim)],
            send_sem=rim_sem.at[0], recv_sem=rim_sem.at[1],
            device_id=(to, f), device_id_type=MESH)

    @pl.when(t > 0)
    def _():
        rim_copy(t - 1).start()

    @pl.when(t == nt - 1)
    def _():
        w[:, samp:] = jnp.zeros((ch_dev, rim), w.dtype)

    taps = filt_t.shape[1]
    ft[...] = jnp.zeros(ft.shape, ft.dtype)
    for g in range(nf):
        for h in range(hops):
            ft[g * blk + h * GW:g * blk + (h + 1) * GW, h * HOP:h * HOP + taps] = (
                filt_t[g * GW:(g + 1) * GW, :])
    load.wait()

    def rowsof(g, b):
        return s.at[g, pl.ds(b * blk, blk), :]

    def first(k, b):
        g = f ^ k
        return pltpu.make_async_remote_copy(
            src_ref=rowsof(g, b), dst_ref=r1.at[f, pl.ds(b * blk, blk), :],
            send_sem=s1_send.at[k, b], recv_sem=s1_recv.at[k, b],
            device_id=(t, g), device_id_type=MESH)

    def features(b, side):
        lo = pl.multiple_of(side * (half * blk), half * blk)
        res = lax.dot_general(
            ft[pl.ds(lo, half * blk), :], w[:, b * hops * HOP:b * hops * HOP + span], NT_DIMS,
            preferred_element_type=jnp.float32).astype(s.dtype)
        for g in range(half):
            s[side * half + g, b * blk:(b + 1) * blk, :] = res[g * blk:(g + 1) * blk]

    ahead = 8
    mine = f // half
    line = [(k, b) for b in range(nb) for p in range(half) for k in (nf - 1 - p, half - 1 - p)]
    for b in range(nb):
        if b == nb - 1:
            @pl.when(t < nt - 1)
            def _():
                rim_copy(t).wait_recv()
        features(b, 1 - mine)
        for at, (k, c) in enumerate(line[:ahead]):
            if c == b and k >= half:
                first(k, b).start()
    for b in range(nb):
        features(b, mine)
        for at, (k, c) in enumerate(line[:ahead]):
            if c == b and 0 < k < half:
                first(k, b).start()

    chans = section.shape[1]
    sec = section[...]
    lane = lax.broadcasted_iota(jnp.int32, (1, chans), 1)
    low = jnp.logical_and(pltpu.roll(sec, 1, 1) == sec, lane > 0)
    high = jnp.logical_and(pltpu.roll(sec, chans - 1, 1) == sec, lane < chans - 1)
    marks[0:1, :] = low.astype(jnp.float32)
    marks[1:2, :] = high.astype(jnp.float32)
    tab = table[...]
    here = lax.broadcasted_iota(jnp.int32, tab.shape, 0) == f
    column = jnp.sum(jnp.where(here, tab, 0).astype(jnp.float32), axis=0, keepdims=True)
    wide = min(chans, 512)
    for c in range(0, chans, wide):
        hot = lax.broadcasted_iota(jnp.int32, (tab.shape[1], wide), 0) == sec[:, c:c + wide]
        marks[2:3, c:c + wide] = jnp.dot(
            column, hot.astype(jnp.float32), preferred_element_type=jnp.float32)
    total = x.shape[0]
    x[0:GW, :] = jnp.zeros((GW, x.shape[1]), x.dtype)
    x[total - GW:total, :] = jnp.zeros((GW, x.shape[1]), x.dtype)

    @pl.when(t == 0)
    def _():
        x[GW:total - GW, 0:LANES] = jnp.zeros((total - 2 * GW, LANES), x.dtype)

    @pl.when(t == nt - 1)
    def _():
        x[GW:total - GW, LANES + rows:] = jnp.zeros((total - 2 * GW, LANES), x.dtype)

    def place(source_t, slot, b):
        return x.at[pl.ds(GW + source_t * part + b * blk, blk), pl.ds(LANES + slot * q, q)]

    def second(k, b, i):
        fb = f ^ k
        gc = fb * nsub + i
        to = gc // ndc
        slot = gc % ndc
        src = (s if k == 0 else r1).at[fb, pl.ds(b * blk, blk), pl.ds(i * q, q)]
        dst = place(t, slot, b)
        sem = x_recv.at[t, slot, b]
        return to, pltpu.make_async_copy(src, dst, sem), pltpu.make_async_remote_copy(
            src_ref=src, dst_ref=dst, send_sem=s2_send.at[k, b, i], recv_sem=sem,
            device_id=(to, f), device_id_type=MESH)

    def halo(k, i, upper):
        fb = f ^ k
        gc = fb * nsub + i
        owner = gc // ndc
        to = owner + 1 if upper else owner - 1
        edge = lax.rem(gc, ndc) == (ndc - 1 if upper else 0)
        there = jnp.logical_and(edge, jnp.logical_and(to >= 0, to < nt))
        column = (i + 1) * q - LANES if upper else i * q
        src = (s if k == 0 else r1).at[fb, :, pl.ds(column, LANES)]
        dst = x.at[pl.ds(GW + t * part, part), pl.ds(0 if upper else LANES + rows, LANES)]
        sem = h_recv.at[t, 0 if upper else 1]
        return there, to, pltpu.make_async_copy(src, dst, sem), pltpu.make_async_remote_copy(
            src_ref=src, dst_ref=dst, send_sem=h_send.at[k, i, 0 if upper else 1], recv_sem=sem,
            device_id=(to, f), device_id_type=MESH)

    sent = [0] * nf
    for at, (k, b) in enumerate(line):
        if k > 0:
            first(k, b).wait_recv()
        if at + ahead < len(line) and line[at + ahead][0] > 0:
            first(*line[at + ahead]).start()
        for i in range(nsub):
            to, local, remote = second(k, b, i)

            @pl.when(to == t)
            def _():
                local.start()

            @pl.when(to != t)
            def _():
                remote.start()

            if sent[k] == nb - 1:
                for upper in (True, False):
                    there, to, local, remote = halo(k, i, upper)

                    @pl.when(jnp.logical_and(there, to == t))
                    def _():
                        local.start()

                    @pl.when(jnp.logical_and(there, to != t))
                    def _():
                        remote.start()
        sent[k] += 1

    for source in range(nt):
        for slot in range(ndc):
            for b in range(nb):
                ref = place(source, slot, b)
                pltpu.make_async_copy(ref, ref, x_recv.at[source, slot, b]).wait()
        for side, there in ((0, t > 0), (1, t < nt - 1)):
            ref = x.at[pl.ds(GW + source * part, part), pl.ds(side * (LANES + rows), LANES)]

            @pl.when(there)
            def _():
                pltpu.make_async_copy(ref, ref, h_recv.at[source, side]).wait()

    run = 8
    deep = (run + 2) * GW
    lb = min(256, rows)
    ow = out.shape[0]
    pack = 2 * run
    start = t * rows

    def conv(step, carry):
        tt = step // (rows // lb)
        l0 = pl.multiple_of((step % (rows // lb)) * lb, lb)
        here = pl.ds(pl.multiple_of(start + l0, lb), lb)
        low, high, pick = marks[0:1, here], marks[1:2, here], marks[2:3, here]
        both = []
        for h in range(2):
            top = pl.multiple_of(tt * (pack * GW) + h * (run * GW), run * GW)
            block = x[pl.ds(top, deep), pl.ds(l0, lb + 2 * LANES)]
            wide = block.astype(jnp.float32)
            before = pltpu.roll(wide, 1, 1)[:, LANES:LANES + lb] * low
            after = pltpu.roll(wide, lb + 2 * LANES - 1, 1)[:, LANES:LANES + lb] * high
            depth = jnp.concatenate(
                [before.astype(x.dtype), block[:, LANES:LANES + lb], after.astype(x.dtype)], axis=0)
            acc = jnp.dot(bands[...], depth, preferred_element_type=jnp.float32)
            n = acc.shape[0] // 2
            res = acc[:n]
            res = jnp.where(pick == 1.0, acc[n:], res)
            both.append(res.reshape(ow, run, lb))
        out[:, pl.ds(pl.multiple_of(tt * pack, pack), pack), pl.ds(l0, lb)] = (
            jnp.concatenate(both, axis=1).astype(out.dtype))
        return carry

    lax.fori_loop(0, (out.shape[1] // pack) * (rows // lb), conv, 0)

    @pl.when(t > 0)
    def _():
        rim_copy(t - 1).wait_send()

    for k in range(nf):
        for b in range(nb):
            if k > 0:
                first(k, b).wait_send()
            for i in range(nsub):
                to, _, remote = second(k, b, i)

                @pl.when(to != t)
                def _():
                    remote.wait_send()
        for i in range(nsub):
            for upper in (True, False):
                there, to, _, remote = halo(k, i, upper)

                @pl.when(jnp.logical_and(there, to != t))
                def _():
                    remote.wait_send()


def shards(nt, nf, waveform, filters, channel_section, section_bank, conv_bank):
    ch_dev, samp = waveform.shape
    taps, nfilt = filters.shape
    rim = taps - HOP
    hops = LANES // GW
    span = rim + hops * HOP
    nb = samp // (HOP * hops)
    blk = hops * GW
    rows = ch_dev * nf // nt
    frames = samp // HOP * nt
    q = min(rows, ch_dev)
    ndc, nsub = rows // q, ch_dev // q
    banks = conv_bank.shape[0]
    run = 8
    base = conv_bank[:, 0].transpose(0, 3, 1, 2, 4).reshape(banks * GW, 3, 3 * GW)
    bands = jnp.stack(
        [jnp.pad(base, ((0, 0), (0, 0), (r * GW, (run - 1 - r) * GW))) for r in range(run)], axis=1
    ).reshape(banks * GW * run, 3 * (run + 2) * GW)
    dt = waveform.dtype
    vmem = pl.BlockSpec(memory_space=pltpu.VMEM)
    dma = pltpu.SemaphoreType.DMA
    events = pl.pallas_call(
        functools.partial(kernel, nt, nf),
        out_shape=jax.ShapeDtypeStruct((GW, frames, rows), dt),
        in_specs=[pl.BlockSpec(memory_space=pl.ANY)] + [vmem] * 4,
        out_specs=vmem,
        scratch_shapes=[
            pltpu.VMEM((ch_dev, samp + rim), dt),
            pltpu.VMEM((nf * blk, span), dt),
            pltpu.VMEM((nf, nb * blk, ch_dev), dt),
            pltpu.VMEM((nf, nb * blk, ch_dev), dt),
            pltpu.VMEM((frames * GW + 2 * GW, rows + 2 * LANES), dt),
            pltpu.VMEM((8, channel_section.shape[0]), jnp.float32),
            dma, dma((2,)), dma((nf, nb)), dma((nf, nb)), dma((nf, nb, nsub)),
            dma((nt, ndc, nb)), dma((nf, nsub, 2)), dma((nt, 2)),
        ],
        compiler_params=pltpu.CompilerParams(
            collective_id=0, has_side_effects=True, vmem_limit_bytes=56 * 1024 * 1024),
    )(waveform, filters.T, bands, channel_section[None, :], section_bank.T)
    return events.transpose(2, 0, 1)


def solution(mesh):
    placed = (P("fiber", "tm"), P(), P(), P(), P(None, "fiber", None, None, None, None))
    return jax.shard_map(
        functools.partial(shards, mesh.shape["tm"], mesh.shape["fiber"]), mesh=mesh,
        in_specs=placed, out_specs=P("tm", "fiber", None), check_vma=False
    )
```
